32 devices in a mesh: group: 2 (over y), expert: 16 (over z, x, core).
Axes of the slice: x: 2, y: 2, z: 4, core: 2. Of those that a mesh axis runs over, the one named last changes fastest.
Arguments:
- values: bfloat16 [128, 7168], P(('group', 'expert')), parts along dimension 0, may hold values from -6 to 6
- scales: float32 [128, 56], P(('group', 'expert')), parts along dimension 0, may hold values from 0.25 to 4
- routes: int32 [128, 8], P(('group', 'expert')), parts along dimension 0, may hold values from 0 to 15, all different within a row; in each aligned block of 4 rows (0 to 3, 4 to 7, ...) at most 3 rows name the same one
- weights: float32 [128, 8], P(('group', 'expert')), parts along dimension 0, may hold values from 0.1 to 1
- w_gate: bfloat16 [7168, 32768], P(None, 'expert'), may hold values from -0.0625 to 0.0625
- w_up: bfloat16 [7168, 32768], P(None, 'expert'), may hold values from -0.0625 to 0.0625
- w_down: bfloat16 [32768, 7168], P('expert'), may hold values from -0.125 to 0.125
Outputs:
- layer_out: bfloat16 [128, 7168], P(('group', 'expert')), parts along dimension 0
The draws below stay inside these ranges and needn't reach their ends.
There are 2 independent parts, one for each index of `group`. The reference program is written for one: setup_inputs(seed, part) draws one part's arguments, and reference() takes and returns one part's arrays. A program takes and returns all parts, laid end to end along the dimension named above; an argument that names none is the same for every part. Nothing has to cross between parts.
Inputs may be any that keep to these rules, and one draw needn't show every extreme that they name: `routes`: each row names 8 different experts; among the 4 rows of one device at most 3 name the same expert, and in every draw some expert is named by exactly 3 rows of some device.
All inputs are finite; a program needn't handle non-finite values.
Results may differ from the reference program's by a relative error of at most 0.019.
Values may be sent and summed in bfloat16 or wider, within the bound.
A program may use at most 192 MiB of HBM per device.

```python
import math
import jax
import jax.numpy as jnp
import numpy as np
from jax import lax

D = 7168
FF = 2048
TOP = 8
BLOCK = 128
EXPERTS = 16
TOK_DEV = 4
CAP = 3
TOKENS = 64


def block_levels(key, dims, shards, low, high):
    level, own = 1.0, jax.random.fold_in(key, 6)
    for position, shards_of in shards:
        heights = jnp.exp(jax.random.uniform(jax.random.fold_in(own, position), (shards_of,), jnp.float32, low / len(shards), high / len(shards)))
        level = level * jnp.repeat(heights, dims[position] // shards_of).reshape([-1 if axis == position else 1 for axis in range(len(dims))])
    return level


def assign_block(rng, own, number, rows, count, top, limit, skew):
    order = jax.random.permutation(rng, count)
    heavy_load, ordinary = shares(count, rows * top, limit, skew, True), shares(count, rows * top, limit, skew, False)
    places = jnp.arange(count)

    def named(sizes, turn):
        used = int((sizes > 0).sum())
        fixed = max(1, used // 4)
        shifted = fixed + (places - fixed + turn * (used - fixed)) % max(1, count - fixed)
        return jnp.zeros((count,), jnp.int32).at[order[jnp.where(places < fixed, places, shifted)]].set(jnp.asarray(sizes, jnp.int32))

    sizes = jnp.where(number % 4 == 0, named(heavy_load, number // 4), named(ordinary, number - number // 4 - 1))
    mixed = jax.random.permutation(jax.random.fold_in(own, 3), count)
    source_of, receiver = mixed[0:count // 2 * 2:2], mixed[1:count // 2 * 2:2]
    margin = jnp.minimum(sizes[source_of] - 1, limit - sizes[receiver]) // 2
    margin = jnp.where((source_of == order[0]) | (receiver == order[0]) | (sizes[receiver] == 0), 0, jnp.maximum(margin, 0))
    shifted = jax.random.randint(jax.random.fold_in(own, 4), (count // 2,), 0, 1 << 20) % (margin + 1)
    sizes = sizes.at[source_of].add(-shifted).at[receiver].add(shifted)
    items = jnp.searchsorted(jnp.cumsum(sizes), jnp.arange(rows * top), side="right").astype(jnp.int32)
    grid = items.reshape(top, rows).T
    grid = grid[jax.random.permutation(jax.random.fold_in(own, 1), rows)]
    turn = jax.random.randint(jax.random.fold_in(own, 2), (rows, 1), 0, top)
    return jnp.take_along_axis(grid, (jnp.arange(top)[None, :] + turn) % top, axis=1)


def shares(number_of, total, bound, lean, full):
    weights = [(1 << 20) // math.isqrt(standing ** lean) + 1 for standing in range(1, number_of + 1)]
    largest = bound if full else min(bound, max(-(-total // number_of), total * weights[0] // sum(weights)))
    least = 1 if total - largest >= number_of - 1 else 0
    counts, surplus = [largest] + [least] * (number_of - 1), total - largest - least * (number_of - 1)
    while surplus > 0:
        movable = [i for i in range(1, number_of) if counts[i] < largest] or [i for i in range(1, number_of) if counts[i] < bound]
        whole, left = sum([weights[i] for i in movable]), surplus
        for i in movable:
            extra = min(bound - counts[i], max(1, left * weights[i] // whole), surplus)
            counts[i] = counts[i] + extra
            surplus = surplus - extra
    return np.array(counts)


def normal_values(own_key, extent, scale, bound, split=(), kind=jnp.bfloat16):
    drawn = scale * jax.random.normal(own_key, extent, jnp.float32)
    if split:
        drawn = drawn * block_levels(own_key, extent, split, -0.22, 0.18)
    return jnp.clip(drawn, -bound, bound).astype(kind)


def setup_inputs(seed: int = 0, part: int = 0) -> dict:
    splits = jax.random.split(jax.random.key(seed), 8)
    own_keys = jax.random.split(jax.random.fold_in(splits[7], part), 8)
    values = normal_values(own_keys[0], (TOKENS, D), 1.0, 6.0, ((0, 16),))
    scales = jnp.clip(jnp.exp(math.log(4.0) - 2.7725887 * jax.random.uniform(own_keys[1], (TOKENS, D // BLOCK), jnp.float32) ** block_levels(own_keys[1], (TOKENS, D // BLOCK), ((0, 16),), -0.2, 0.2)), 0.25, 4.0)
    routes_keys = jax.random.split(jax.random.fold_in(own_keys[2], 1), TOKENS // TOK_DEV)
    routes_turns = jax.random.permutation(jax.random.fold_in(own_keys[2], 3), TOKENS // TOK_DEV)
    routes = jax.vmap(lambda own, number: assign_block(jax.random.fold_in(own_keys[2], 2), own, number, TOK_DEV, EXPERTS, TOP, CAP, 2))(routes_keys, routes_turns).reshape((TOKENS, TOP))
    weights = jnp.clip(jnp.exp(math.log(1.0) - 2.3025851 * jax.random.uniform(own_keys[3], (TOKENS, TOP), jnp.float32) ** block_levels(own_keys[3], (TOKENS, TOP), ((0, 16),), -0.2, 0.2)), 0.1, 1.0)
    w_gate = normal_values(splits[4], (D, EXPERTS * FF), D ** -0.5, 0.0625, ((1, 16),))
    w_up = normal_values(splits[5], (D, EXPERTS * FF), D ** -0.5, 0.0625, ((1, 16),))
    w_down = normal_values(splits[6], (EXPERTS * FF, D), FF ** -0.5, 0.125, ((0, 16),))
    return {"values": values, "scales": scales, "routes": routes, "weights": weights, "w_gate": w_gate, "w_up": w_up, "w_down": w_down}


def reference(values, scales, routes, weights, w_gate, w_up, w_down):
    dequant = (values.astype(jnp.float32).reshape(TOKENS, D // BLOCK, BLOCK) * scales[:, :, None]).reshape(TOKENS, D).astype(jnp.bfloat16)
    gate_all = w_gate.reshape(D, EXPERTS, FF).transpose(1, 0, 2)
    up_all = w_up.reshape(D, EXPERTS, FF).transpose(1, 0, 2)
    down_all = w_down.reshape(EXPERTS, FF, D)
    expert_ids = jnp.arange(EXPERTS, dtype=jnp.int32)
    route_w = jnp.sum(weights[:, :, None] * (routes[:, :, None] == expert_ids[None, None, :]).astype(jnp.float32), axis=1)

    def expert_step(running, expert_items):
        gate_w, up_w, down_w, column = expert_items
        gate_proj = jnp.dot(dequant, gate_w, preferred_element_type=jnp.float32)
        up_proj = jnp.dot(dequant, up_w, preferred_element_type=jnp.float32)
        hidden = (jax.nn.silu(gate_proj) * up_proj).astype(jnp.bfloat16)
        output = jnp.dot(hidden, down_w, preferred_element_type=jnp.float32)
        contrib = (column[:, None] * output).astype(jnp.bfloat16)
        return running + contrib.astype(jnp.float32), None

    running, _ = lax.scan(expert_step, jnp.zeros((TOKENS, D), jnp.float32), (gate_all, up_all, down_all, route_w.T))
    return running.astype(jnp.bfloat16)
```

```python
import functools
import jax
import jax.numpy as jnp
from jax import lax
from jax.experimental import pallas as pl
from jax.experimental.pallas import tpu as pltpu
from jax.sharding import PartitionSpec as P

BLOCK = 128
EXPERTS = 16
LANES = 128
MESH = pl.DeviceIdType.MESH
CHUNK = 1024


def kernel(
    outer, group_size, tok, width, ffh,
    values, scales, routes, weights, wg_hbm, wu_hbm, wd_hbm, out,
    zb, x, wg, wu, wd, accg, accu, hid, wcol, tmp, r1, r2a, r2b, r3a, r3b, zret,
    wsem, ssem, rsem,
):
    g = lax.axis_index("group")
    e = lax.axis_index("expert")
    zi, xi, ci = e // 4, (e // 2) % 2, e % 2
    rows = tok * outer
    total = 8 * rows
    nk = width // CHUNK
    cut = CHUNK * ((nk + 1) // 2)
    dispatch = [(0, cut, range(0, cut // CHUNK)), (cut, width + LANES, range(cut // CHUNK, nk))]
    mblk = min(total, 128)
    ntile = min(256, ffh)

    peer_x = (g, zi * 4 + (1 - xi) * 2 + ci)
    peer_y = (1 - g, e)
    peer_c = (g, zi * 4 + xi * 2 + (1 - ci))

    def peer_z(p):
        return (g, lax.rem(zi + p, outer) * 4 + xi * 2 + ci)

    def weight_copies(j):
        half = pl.ds(pl.multiple_of(g * ffh, ffh), ffh)
        part = pl.ds(j * CHUNK, CHUNK)
        return (
            pltpu.make_async_copy(wg_hbm.at[part, half], wg.at[j], wsem.at[0, j]),
            pltpu.make_async_copy(wu_hbm.at[part, half], wu.at[j], wsem.at[1, j]),
            pltpu.make_async_copy(wd_hbm.at[half, part], wd.at[j], wsem.at[2, j]),
        )

    copies = [weight_copies(j) for j in range(nk)]
    for j in range(nk):
        copies[j][0].start()
        copies[j][1].start()
    for j in range(nk):
        copies[j][2].start()

    barrier = pltpu.get_barrier_semaphore()
    for dev in [peer_x, peer_y, peer_c] + [peer_z(p) for p in range(1, outer)]:
        pl.semaphore_signal(barrier, inc=1, device_id=dev, device_id_type=MESH)

    for b in range(width // BLOCK):
        cols = slice(b * BLOCK, (b + 1) * BLOCK)
        row = values[:, cols].astype(jnp.float32) * scales[:, b : b + 1]
        zb[zi, :, cols] = row.astype(jnp.bfloat16)
    lane = lax.broadcasted_iota(jnp.int32, (tok, LANES), 1)
    rw = jnp.zeros((tok, LANES), jnp.float32)
    low_lane = jnp.where(lane < 64, lane, lane - 64)
    for k in range(routes.shape[1]):
        rw = rw + jnp.where(low_lane == routes[:, k : k + 1], weights[:, k : k + 1], 0.0)
    high = rw.astype(jnp.bfloat16).astype(jnp.float32)
    zb[zi, :, width:] = jnp.where(lane < 64, high, rw - high).astype(jnp.bfloat16)

    pl.semaphore_wait(barrier, 3 + outer - 1)

    count = [0]
    sent = []

    def move(src, dst, dev):
        n = count[0]
        count[0] += 1
        copy = pltpu.make_async_remote_copy(
            src_ref=src, dst_ref=dst, send_sem=ssem.at[n], recv_sem=rsem.at[n],
            device_id=dev, device_id_type=MESH,
        )
        sent.append(copy)
        return copy

    def landed(view, copy_index):
        pltpu.make_async_remote_copy(
            src_ref=view, dst_ref=view, send_sem=ssem.at[copy_index],
            recv_sem=rsem.at[copy_index], device_id=peer_c, device_id_type=MESH,
        ).wait_recv()

    def block(c, y, xx, c0, c1):
        start = pl.multiple_of((c * 4 + y * 2 + xx) * rows, 16)
        return x.at[pl.ds(start, rows), pl.ds(c0, c1 - c0)]

    def push(view, dev):
        copy = move(view, view, dev)
        copy.start()
        return count[0] - 1

    zid = []
    for c0, c1, _ in dispatch:
        ids = []
        for p in range(1, outer):
            ids.append(push(zb.at[zi, :, pl.ds(c0, c1 - c0)], peer_z(p)))
        zid.append(ids)
    second = []
    for d, (c0, c1, _) in enumerate(dispatch):
        for p in range(1, outer):
            source = lax.rem(zi - p + outer, outer)
            landed(zb.at[source, :, pl.ds(c0, c1 - c0)], zid[d][p - 1])
        for z in range(outer):
            tmp[z * tok : (z + 1) * tok, : c1 - c0] = zb[z, :, c0:c1].astype(jnp.float32)
        start = pl.multiple_of((ci * 4 + g * 2 + xi) * rows, 16)
        x[pl.ds(start, rows), c0:c1] = tmp[:, : c1 - c0].astype(jnp.bfloat16)
        mine = block(ci, g, xi, c0, c1)
        second.append((push(mine, peer_x), push(mine, peer_y), push(mine, peer_c)))
    third = []
    for d, (c0, c1, _) in enumerate(dispatch):
        mid = (c0 + c1) // 2 // 128 * 128
        landed(block(ci, g, 1 - xi, c0, c1), second[d][0])
        a = push(block(ci, g, 1 - xi, c0, mid), peer_y)
        ca = push(block(ci, g, 1 - xi, c0, c1), peer_c)
        landed(block(ci, 1 - g, xi, c0, c1), second[d][1])
        b = push(block(ci, 1 - g, xi, mid, c1), peer_x)
        cb = push(block(ci, 1 - g, xi, c0, c1), peer_c)
        third.append((a, b, ca, cb))
    fourth = []
    for d, (c0, c1, _) in enumerate(dispatch):
        mid = (c0 + c1) // 2 // 128 * 128
        landed(block(ci, 1 - g, 1 - xi, c0, mid), third[d][0])
        fa = push(block(ci, 1 - g, 1 - xi, c0, mid), peer_c)
        landed(block(ci, 1 - g, 1 - xi, mid, c1), third[d][1])
        fb = push(block(ci, 1 - g, 1 - xi, mid, c1), peer_c)
        fourth.append((fa, fb))

    accg[...] = jnp.zeros_like(accg)
    accu[...] = jnp.zeros_like(accu)
    for d, (c0, c1, chunks) in enumerate(dispatch):
        mid = (c0 + c1) // 2 // 128 * 128
        oc = 1 - ci
        landed(block(oc, g, xi, c0, c1), second[d][2])
        landed(block(oc, g, 1 - xi, c0, c1), third[d][2])
        landed(block(oc, 1 - g, xi, c0, c1), third[d][3])
        landed(block(oc, 1 - g, 1 - xi, c0, mid), fourth[d][0])
        landed(block(oc, 1 - g, 1 - xi, mid, c1), fourth[d][1])
        for j in chunks:
            copies[j][0].wait()
            copies[j][1].wait()

            @pl.loop(0, total // mblk)
            def _(m):
                at = pl.ds(pl.multiple_of(m * mblk, mblk), mblk)
                lhs = x[at, j * CHUNK : (j + 1) * CHUNK]

                @pl.loop(0, ffh // ntile)
                def _(n):
                    cols = pl.ds(pl.multiple_of(n * ntile, ntile), ntile)
                    accg[at, cols] += jnp.dot(
                        lhs, wg[j, :, cols], preferred_element_type=jnp.float32
                    )
                    accu[at, cols] += jnp.dot(
                        lhs, wu[j, :, cols], preferred_element_type=jnp.float32
                    )

    mine_e = e // group_size

    @pl.loop(0, total // mblk)
    def _(m):
        at = pl.ds(pl.multiple_of(m * mblk, mblk), mblk)
        gate = accg[at, :]
        hid[at, :] = (gate / (1.0 + jnp.exp(-gate)) * accu[at, :]).astype(jnp.bfloat16)
        wide = x[at, width:].astype(jnp.float32)
        lanes = lax.broadcasted_iota(jnp.int32, (mblk, LANES), 1)
        keep = (lanes == mine_e) | (lanes == mine_e + 64)
        column = jnp.sum(jnp.where(keep, wide, 0.0), axis=1, keepdims=True)
        wcol[at, :] = jnp.broadcast_to(column, (mblk, LANES))

    for copy in sent:
        copy.wait_send()
    sent.clear()

    own = pl.ds(pl.multiple_of(ci * 4 * rows, 16), 4 * rows)
    other = pl.ds(pl.multiple_of((1 - ci) * 4 * rows, 16), 4 * rows)
    half = CHUNK // 2
    ids = [dict() for _ in range(nk)]
    dtile = 256

    def stage_down(j):
        copies[j][2].wait()

        @pl.loop(0, total // mblk)
        def _(m):
            at = pl.ds(pl.multiple_of(m * mblk, mblk), mblk)

            @pl.loop(0, CHUNK // dtile)
            def _(n):
                cols = pl.ds(pl.multiple_of(n * dtile, dtile), dtile)
                to = pl.ds(pl.multiple_of(j * CHUNK + n * dtile, dtile), dtile)
                got = jnp.dot(hid[at, :], wd[j, :, cols], preferred_element_type=jnp.float32)
                x[at, to] = (got * wcol[at, 0:1]).astype(jnp.bfloat16)

        cols = pl.ds(j * CHUNK, CHUNK)
        move(x.at[other, cols], r1.at[:, cols], peer_c).start()
        ids[j]["c"] = count[0] - 1

    def stage_core(j):
        cols = pl.ds(j * CHUNK, CHUNK)
        landed(r1.at[:, cols], ids[j]["c"])
        both = x[own, cols].astype(jnp.float32) + r1[:, cols].astype(jnp.float32)
        r1[:, cols] = both.astype(jnp.bfloat16)
        a, b = pl.ds(j * CHUNK, half), pl.ds(j * CHUNK + half, half)
        h = pl.ds(j * half, half)
        for y in range(2):
            start = pl.multiple_of((y * 2 + 1 - xi) * rows, 16)
            move(r1.at[pl.ds(start, rows), a], r2a.at[y, :, h], peer_x).start()
            ids[j]["x%d" % y] = count[0] - 1
        start = pl.multiple_of((1 - g) * 2 * rows, 16)
        move(r1.at[pl.ds(start, 2 * rows), b], r2b.at[:, h], peer_y).start()
        ids[j]["y"] = count[0] - 1

    def stage_plane(j):
        a, b = pl.ds(j * CHUNK, half), pl.ds(j * CHUNK + half, half)
        h = pl.ds(j * half, half)
        for y in range(2):
            landed(r2a.at[y, :, h], ids[j]["x%d" % y])
            start = pl.multiple_of((y * 2 + xi) * rows, 16)
            both = r1[pl.ds(start, rows), a].astype(jnp.float32) + r2a[y, :, h].astype(jnp.float32)
            r2a[y, :, h] = both.astype(jnp.bfloat16)
        move(r2a.at[1 - g, :, h], r3a.at[:, h], peer_y).start()
        ids[j]["a"] = count[0] - 1
        landed(r2b.at[:, h], ids[j]["y"])
        start = pl.multiple_of(g * 2 * rows, 16)
        both = r1[pl.ds(start, 2 * rows), b].astype(jnp.float32) + r2b[:, h].astype(jnp.float32)
        r2b[:, h] = both.astype(jnp.bfloat16)
        start = pl.multiple_of((1 - xi) * rows, 16)
        move(r2b.at[pl.ds(start, rows), h], r3b.at[:, h], peer_x).start()
        ids[j]["b"] = count[0] - 1

    def stage_line(j):
        h = pl.ds(j * half, half)
        landed(r3a.at[:, h], ids[j]["a"])
        tmp[:, 0:half] = r2a[g, :, h].astype(jnp.float32) + r3a[:, h].astype(jnp.float32)
        landed(r3b.at[:, h], ids[j]["b"])
        start = pl.multiple_of(xi * rows, 16)
        tmp[:, half:CHUNK] = (
            r2b[pl.ds(start, rows), h].astype(jnp.float32) + r3b[:, h].astype(jnp.float32)
        )
        cols = pl.ds(j * CHUNK, CHUNK)
        for z in range(outer):
            zb[z, :, cols] = tmp[z * tok : (z + 1) * tok, 0:CHUNK].astype(jnp.bfloat16)
        ids[j]["z"] = []
        for p in range(1, outer):
            to = lax.rem(zi + p, outer)
            move(zb.at[to, :, cols], zret.at[zi, :, cols], peer_z(p)).start()
            ids[j]["z"].append(count[0] - 1)

    def stage_out(j):
        cols = pl.ds(j * CHUNK, CHUNK)
        sums = zb[zi, :, cols].astype(jnp.float32)
        for p in range(1, outer):
            source = lax.rem(zi - p + outer, outer)
            landed(zret.at[source, :, cols], ids[j]["z"][p - 1])
            sums = sums + zret[source, :, cols].astype(jnp.float32)
        out[:, cols] = sums.astype(jnp.bfloat16)

    stages = (stage_down, stage_core, stage_plane, stage_line, stage_out)
    for step in range(nk + len(stages) - 1):
        for s, stage in enumerate(stages):
            if 0 <= step - s < nk:
                stage(step - s)
    for copy in sent:
        copy.wait_send()


def body(values, scales, routes, weights, w_gate, w_up, w_down):
    devices = lax.axis_size("expert")
    outer = devices // 4
    tok, width = values.shape
    ffh = w_gate.shape[1] // 2
    rows = tok * outer
    nk = width // CHUNK
    bf, f32 = jnp.bfloat16, jnp.float32
    n_copies = 2 * (outer - 1 + 9) + nk * (6 + outer - 1)
    vmem = pl.BlockSpec(memory_space=pltpu.VMEM)
    hbm = pl.BlockSpec(memory_space=pl.ANY)
    macs = 8 * rows * width * ffh * 3
    return pl.pallas_call(
        functools.partial(kernel, outer, devices // EXPERTS, tok, width, ffh),
        out_shape=jax.ShapeDtypeStruct((tok, width), bf),
        in_specs=[vmem] * 4 + [hbm] * 3,
        out_specs=vmem,
        scratch_shapes=[
            pltpu.VMEM((outer, tok, width + LANES), bf),
            pltpu.VMEM((8 * rows, width + LANES), bf),
            pltpu.VMEM((nk, CHUNK, ffh), bf),
            pltpu.VMEM((nk, CHUNK, ffh), bf),
            pltpu.VMEM((nk, ffh, CHUNK), bf),
            pltpu.VMEM((8 * rows, ffh), f32),
            pltpu.VMEM((8 * rows, ffh), f32),
            pltpu.VMEM((8 * rows, ffh), bf),
            pltpu.VMEM((8 * rows, LANES), f32),
            pltpu.VMEM((rows, CHUNK * ((nk + 1) // 2)), f32),
            pltpu.VMEM((4 * rows, width), bf),
            pltpu.VMEM((2, rows, width // 2), bf),
            pltpu.VMEM((2 * rows, width // 2), bf),
            pltpu.VMEM((rows, width // 2), bf),
            pltpu.VMEM((rows, width // 2), bf),
            pltpu.VMEM((outer, tok, width), bf),
            pltpu.SemaphoreType.DMA((3, nk)),
            pltpu.SemaphoreType.DMA((n_copies,)),
            pltpu.SemaphoreType.DMA((n_copies,)),
        ],
        compiler_params=pltpu.CompilerParams(
            collective_id=0, has_side_effects=True, vmem_limit_bytes=60 * 2**20
        ),
        cost_estimate=pl.CostEstimate(
            flops=2 * macs, bytes_accessed=6 * width * ffh, transcendentals=8 * rows * ffh
        ),
    )(values, scales, routes, weights, w_gate, w_up, w_down)


def solution(mesh):
    return jax.shard_map(
        body,
        mesh=mesh,
        in_specs=(
            P(("group", "expert"), None),
            P(("group", "expert"), None),
            P(("group", "expert"), None),
            P(("group", "expert"), None),
            P(None, "expert"),
            P(None, "expert"),
            P("expert", None),
        ),
        out_specs=P(("group", "expert"), None),
        check_vma=False,
    )
```

```python
import functools
import jax
import jax.numpy as jnp
from jax import lax
from jax.experimental import pallas as pl
from jax.experimental.pallas import tpu as pltpu
from jax.sharding import PartitionSpec as P

BLOCK = 128
EXPERTS = 16
LANES = 128
MESH = pl.DeviceIdType.MESH
CHUNK = 1024
GATHER_LAG = 3
RETURN_LAG = 3
TILE = 1024


def kernel(
    outer, group_size, tok, width, ffh,
    values, scales, routes, weights, wg_hbm, wu_hbm, wd_hbm, out,
    zb, x, wg, wu, wd, accg, accu, hid, wcol, tmp, r1, r2a, r2b, r3a, r3b, zret,
    wsem, ssem, rsem,
):
    g = lax.axis_index("group")
    e = lax.axis_index("expert")
    zi, xi, ci = e // 4, (e // 2) % 2, e % 2
    rows = tok * outer
    total = 8 * rows
    nk = width // CHUNK
    edges = [(j * CHUNK, (j + 1) * CHUNK + (LANES if j == nk - 1 else 0)) for j in range(nk)]
    mblk = min(total, 128)
    ntile = min(TILE, ffh)

    peer_x = (g, zi * 4 + (1 - xi) * 2 + ci)
    peer_y = (1 - g, e)
    peer_c = (g, zi * 4 + xi * 2 + (1 - ci))

    def peer_z(p):
        return (g, lax.rem(zi + p, outer) * 4 + xi * 2 + ci)

    def weight_copies(j):
        half = pl.ds(pl.multiple_of(g * ffh, ffh), ffh)
        part = pl.ds(j * CHUNK, CHUNK)
        return (
            pltpu.make_async_copy(wg_hbm.at[part, half], wg.at[j], wsem.at[0, j]),
            pltpu.make_async_copy(wu_hbm.at[part, half], wu.at[j], wsem.at[1, j]),
            pltpu.make_async_copy(wd_hbm.at[half, part], wd.at[j], wsem.at[2, j]),
        )

    copies = [weight_copies(j) for j in range(nk)]
    for j in range(nk):
        copies[j][0].start()
        copies[j][1].start()
    for j in range(nk):
        copies[j][2].start()

    barrier = pltpu.get_barrier_semaphore()
    for dev in [peer_x, peer_y, peer_c] + [peer_z(p) for p in range(1, outer)]:
        pl.semaphore_signal(barrier, inc=1, device_id=dev, device_id_type=MESH)

    for b in range(width // BLOCK):
        cols = slice(b * BLOCK, (b + 1) * BLOCK)
        row = values[:, cols].astype(jnp.float32) * scales[:, b : b + 1]
        zb[zi, :, cols] = row.astype(jnp.bfloat16)
    lane = lax.broadcasted_iota(jnp.int32, (tok, LANES), 1)
    rw = jnp.zeros((tok, LANES), jnp.float32)
    low_lane = jnp.where(lane < 64, lane, lane - 64)
    for k in range(routes.shape[1]):
        rw = rw + jnp.where(low_lane == routes[:, k : k + 1], weights[:, k : k + 1], 0.0)
    high = rw.astype(jnp.bfloat16).astype(jnp.float32)
    zb[zi, :, width:] = jnp.where(lane < 64, high, rw - high).astype(jnp.bfloat16)

    pl.semaphore_wait(barrier, 3 + outer - 1)

    count = [0]
    sent = []

    def move(src, dst, dev):
        n = count[0]
        count[0] += 1
        copy = pltpu.make_async_remote_copy(
            src_ref=src, dst_ref=dst, send_sem=ssem.at[n], recv_sem=rsem.at[n],
            device_id=dev, device_id_type=MESH,
        )
        sent.append(copy)
        return copy

    def landed(view, copy_index):
        pltpu.make_async_remote_copy(
            src_ref=view, dst_ref=view, send_sem=ssem.at[copy_index],
            recv_sem=rsem.at[copy_index], device_id=peer_c, device_id_type=MESH,
        ).wait_recv()

    def block(c, y, xx, c0, c1):
        start = pl.multiple_of((c * 4 + y * 2 + xx) * rows, 16)
        return x.at[pl.ds(start, rows), pl.ds(c0, c1 - c0)]

    def push(view, dev):
        copy = move(view, view, dev)
        copy.start()
        return count[0] - 1

    zid = []
    for c0, c1 in edges:
        ids = []
        for p in range(1, outer):
            ids.append(push(zb.at[zi, :, pl.ds(c0, c1 - c0)], peer_z(p)))
        zid.append(ids)
    second, third, fourth = [], [], []

    def gather_line(d):
        c0, c1 = edges[d]
        for p in range(1, outer):
            source = lax.rem(zi - p + outer, outer)
            landed(zb.at[source, :, pl.ds(c0, c1 - c0)], zid[d][p - 1])
        for z in range(outer):
            tmp[z * tok : (z + 1) * tok, : c1 - c0] = zb[z, :, c0:c1].astype(jnp.float32)
        start = pl.multiple_of((ci * 4 + g * 2 + xi) * rows, 16)
        x[pl.ds(start, rows), c0:c1] = tmp[:, : c1 - c0].astype(jnp.bfloat16)
        mine = block(ci, g, xi, c0, c1)
        second.append((push(mine, peer_x), push(mine, peer_y), push(mine, peer_c)))

    def gather_plane(d):
        c0, c1 = edges[d]
        mid = c0 + CHUNK // 2
        landed(block(ci, g, 1 - xi, c0, c1), second[d][0])
        a = push(block(ci, g, 1 - xi, c0, mid), peer_y)
        ca = push(block(ci, g, 1 - xi, c0, c1), peer_c)
        landed(block(ci, 1 - g, xi, c0, c1), second[d][1])
        b = push(block(ci, 1 - g, xi, mid, c1), peer_x)
        cb = push(block(ci, 1 - g, xi, c0, c1), peer_c)
        third.append((a, b, ca, cb))

    def gather_corner(d):
        c0, c1 = edges[d]
        mid = c0 + CHUNK // 2
        landed(block(ci, 1 - g, 1 - xi, c0, mid), third[d][0])
        fa = push(block(ci, 1 - g, 1 - xi, c0, mid), peer_c)
        landed(block(ci, 1 - g, 1 - xi, mid, c1), third[d][1])
        fb = push(block(ci, 1 - g, 1 - xi, mid, c1), peer_c)
        fourth.append((fa, fb))

    def project(d):
        c0, c1 = edges[d]
        mid = c0 + CHUNK // 2
        oc = 1 - ci
        landed(block(oc, g, xi, c0, c1), second[d][2])
        landed(block(oc, g, 1 - xi, c0, c1), third[d][2])
        landed(block(oc, 1 - g, xi, c0, c1), third[d][3])
        landed(block(oc, 1 - g, 1 - xi, c0, mid), fourth[d][0])
        landed(block(oc, 1 - g, 1 - xi, mid, c1), fourth[d][1])
        copies[d][0].wait()
        copies[d][1].wait()

        @pl.loop(0, total // mblk)
        def _(m):
            at = pl.ds(pl.multiple_of(m * mblk, mblk), mblk)
            lhs = x[at, c0 : c0 + CHUNK]

            @pl.loop(0, ffh // ntile)
            def _(n):
                cols = pl.ds(pl.multiple_of(n * ntile, ntile), ntile)
                gate = jnp.dot(lhs, wg[d, :, cols], preferred_element_type=jnp.float32)
                up = jnp.dot(lhs, wu[d, :, cols], preferred_element_type=jnp.float32)
                if d == 0:
                    accg[at, cols] = gate
                    accu[at, cols] = up
                else:
                    accg[at, cols] += gate
                    accu[at, cols] += up

    def run(stages, lag):
        for step in range(nk + (len(stages) - 1) * lag):
            for s, stage in enumerate(stages):
                if 0 <= step - s * lag < nk:
                    stage(step - s * lag)

    run((gather_line, gather_plane, gather_corner, project), GATHER_LAG)

    mine_e = e // group_size

    @pl.loop(0, total // mblk)
    def _(m):
        at = pl.ds(pl.multiple_of(m * mblk, mblk), mblk)
        gate = accg[at, :]
        hid[at, :] = (gate / (1.0 + jnp.exp(-gate)) * accu[at, :]).astype(jnp.bfloat16)
        wide = x[at, width:].astype(jnp.float32)
        lanes = lax.broadcasted_iota(jnp.int32, (mblk, LANES), 1)
        keep = (lanes == mine_e) | (lanes == mine_e + 64)
        column = jnp.sum(jnp.where(keep, wide, 0.0), axis=1, keepdims=True)
        wcol[at, :] = jnp.broadcast_to(column, (mblk, LANES))

    for copy in sent:
        copy.wait_send()
    sent.clear()

    own = pl.ds(pl.multiple_of(ci * 4 * rows, 16), 4 * rows)
    other = pl.ds(pl.multiple_of((1 - ci) * 4 * rows, 16), 4 * rows)
    half = CHUNK // 2
    ids = [dict() for _ in range(nk)]
    dtile = TILE

    def stage_down(j):
        copies[j][2].wait()

        @pl.loop(0, total // mblk)
        def _(m):
            at = pl.ds(pl.multiple_of(m * mblk, mblk), mblk)

            @pl.loop(0, CHUNK // dtile)
            def _(n):
                cols = pl.ds(pl.multiple_of(n * dtile, dtile), dtile)
                to = pl.ds(pl.multiple_of(j * CHUNK + n * dtile, dtile), dtile)
                got = jnp.dot(hid[at, :], wd[j, :, cols], preferred_element_type=jnp.float32)
                x[at, to] = (got * wcol[at, 0:1]).astype(jnp.bfloat16)

        cols = pl.ds(j * CHUNK, CHUNK)
        move(x.at[other, cols], r1.at[:, cols], peer_c).start()
        ids[j]["c"] = count[0] - 1

    def stage_core(j):
        cols = pl.ds(j * CHUNK, CHUNK)
        landed(r1.at[:, cols], ids[j]["c"])
        both = x[own, cols].astype(jnp.float32) + r1[:, cols].astype(jnp.float32)
        r1[:, cols] = both.astype(jnp.bfloat16)
        a, b = pl.ds(j * CHUNK, half), pl.ds(j * CHUNK + half, half)
        h = pl.ds(j * half, half)
        for y in range(2):
            start = pl.multiple_of((y * 2 + 1 - xi) * rows, 16)
            move(r1.at[pl.ds(start, rows), a], r2a.at[y, :, h], peer_x).start()
            ids[j]["x%d" % y] = count[0] - 1
        start = pl.multiple_of((1 - g) * 2 * rows, 16)
        move(r1.at[pl.ds(start, 2 * rows), b], r2b.at[:, h], peer_y).start()
        ids[j]["y"] = count[0] - 1

    def stage_plane(j):
        a, b = pl.ds(j * CHUNK, half), pl.ds(j * CHUNK + half, half)
        h = pl.ds(j * half, half)
        for y in range(2):
            landed(r2a.at[y, :, h], ids[j]["x%d" % y])
            start = pl.multiple_of((y * 2 + xi) * rows, 16)
            both = r1[pl.ds(start, rows), a].astype(jnp.float32) + r2a[y, :, h].astype(jnp.float32)
            r2a[y, :, h] = both.astype(jnp.bfloat16)
        move(r2a.at[1 - g, :, h], r3a.at[:, h], peer_y).start()
        ids[j]["a"] = count[0] - 1
        landed(r2b.at[:, h], ids[j]["y"])
        start = pl.multiple_of(g * 2 * rows, 16)
        both = r1[pl.ds(start, 2 * rows), b].astype(jnp.float32) + r2b[:, h].astype(jnp.float32)
        r2b[:, h] = both.astype(jnp.bfloat16)
        start = pl.multiple_of((1 - xi) * rows, 16)
        move(r2b.at[pl.ds(start, rows), h], r3b.at[:, h], peer_x).start()
        ids[j]["b"] = count[0] - 1

    def stage_line(j):
        h = pl.ds(j * half, half)
        landed(r3a.at[:, h], ids[j]["a"])
        tmp[:, 0:half] = r2a[g, :, h].astype(jnp.float32) + r3a[:, h].astype(jnp.float32)
        landed(r3b.at[:, h], ids[j]["b"])
        start = pl.multiple_of(xi * rows, 16)
        tmp[:, half:CHUNK] = (
            r2b[pl.ds(start, rows), h].astype(jnp.float32) + r3b[:, h].astype(jnp.float32)
        )
        cols = pl.ds(j * CHUNK, CHUNK)
        for z in range(outer):
            zb[z, :, cols] = tmp[z * tok : (z + 1) * tok, 0:CHUNK].astype(jnp.bfloat16)
        ids[j]["z"] = []
        for p in range(1, outer):
            to = lax.rem(zi + p, outer)
            move(zb.at[to, :, cols], zret.at[zi, :, cols], peer_z(p)).start()
            ids[j]["z"].append(count[0] - 1)

    def stage_out(j):
        cols = pl.ds(j * CHUNK, CHUNK)
        sums = zb[zi, :, cols].astype(jnp.float32)
        for p in range(1, outer):
            source = lax.rem(zi - p + outer, outer)
            landed(zret.at[source, :, cols], ids[j]["z"][p - 1])
            sums = sums + zret[source, :, cols].astype(jnp.float32)
        out[:, cols] = sums.astype(jnp.bfloat16)

    run((stage_down, stage_core, stage_plane, stage_line, stage_out), RETURN_LAG)
    for copy in sent:
        copy.wait_send()


def body(values, scales, routes, weights, w_gate, w_up, w_down):
    devices = lax.axis_size("expert")
    outer = devices // 4
    tok, width = values.shape
    ffh = w_gate.shape[1] // 2
    rows = tok * outer
    nk = width // CHUNK
    bf, f32 = jnp.bfloat16, jnp.float32
    n_copies = nk * (outer - 1 + 9) + nk * (6 + outer - 1)
    vmem = pl.BlockSpec(memory_space=pltpu.VMEM)
    hbm = pl.BlockSpec(memory_space=pl.ANY)
    macs = 8 * rows * width * ffh * 3
    return pl.pallas_call(
        functools.partial(kernel, outer, devices // EXPERTS, tok, width, ffh),
        out_shape=jax.ShapeDtypeStruct((tok, width), bf),
        in_specs=[vmem] * 4 + [hbm] * 3,
        out_specs=vmem,
        scratch_shapes=[
            pltpu.VMEM((outer, tok, width + LANES), bf),
            pltpu.VMEM((8 * rows, width + LANES), bf),
            pltpu.VMEM((nk, CHUNK, ffh), bf),
            pltpu.VMEM((nk, CHUNK, ffh), bf),
            pltpu.VMEM((nk, ffh, CHUNK), bf),
            pltpu.VMEM((8 * rows, ffh), f32),
            pltpu.VMEM((8 * rows, ffh), f32),
            pltpu.VMEM((8 * rows, ffh), bf),
            pltpu.VMEM((8 * rows, LANES), f32),
            pltpu.VMEM((rows, CHUNK + LANES), f32),
            pltpu.VMEM((4 * rows, width), bf),
            pltpu.VMEM((2, rows, width // 2), bf),
            pltpu.VMEM((2 * rows, width // 2), bf),
            pltpu.VMEM((rows, width // 2), bf),
            pltpu.VMEM((rows, width // 2), bf),
            pltpu.VMEM((outer, tok, width), bf),
            pltpu.SemaphoreType.DMA((3, nk)),
            pltpu.SemaphoreType.DMA((n_copies,)),
            pltpu.SemaphoreType.DMA((n_copies,)),
        ],
        compiler_params=pltpu.CompilerParams(
            collective_id=0, has_side_effects=True, vmem_limit_bytes=60 * 2**20
        ),
        cost_estimate=pl.CostEstimate(
            flops=2 * macs, bytes_accessed=6 * width * ffh, transcendentals=8 * rows * ffh
        ),
    )(values, scales, routes, weights, w_gate, w_up, w_down)


def solution(mesh):
    return jax.shard_map(
        body,
        mesh=mesh,
        in_specs=(
            P(("group", "expert"), None),
            P(("group", "expert"), None),
            P(("group", "expert"), None),
            P(("group", "expert"), None),
            P(None, "expert"),
            P(None, "expert"),
            P("expert", None),
        ),
        out_specs=P(("group", "expert"), None),
        check_vma=False,
    )
```

```python
import functools
import jax
import jax.numpy as jnp
from jax import lax
from jax.experimental import pallas as pl
from jax.experimental.pallas import tpu as pltpu
from jax.sharding import PartitionSpec as P

BLOCK = 128
EXPERTS = 16
LANES = 128
MESH = pl.DeviceIdType.MESH
CHUNK = 1024
GATHER_LAG = 3
RETURN_LAG = 4
TILE = 1024


def kernel(
    outer, group_size, tok, width, ffh,
    values, scales, routes, weights, wg_hbm, wu_hbm, wd_hbm, out,
    zb, x, wg, wu, wd, accg, accu, hid, wcol, tmp, r1, r2a, r2b, r3a, r3b, zret,
    wsem, ssem, rsem,
):
    g = lax.axis_index("group")
    e = lax.axis_index("expert")
    zi, xi, ci = e // 4, (e // 2) % 2, e % 2
    rows = tok * outer
    total = 8 * rows
    nk = width // CHUNK
    edges = [(j * CHUNK, (j + 1) * CHUNK + (LANES if j == nk - 1 else 0)) for j in range(nk)]
    mblk = min(total, 128)
    ntile = min(TILE, ffh)

    peer_x = (g, zi * 4 + (1 - xi) * 2 + ci)
    peer_y = (1 - g, e)
    peer_c = (g, zi * 4 + xi * 2 + (1 - ci))

    def peer_z(p):
        return (g, lax.rem(zi + p, outer) * 4 + xi * 2 + ci)

    def weight_copies(j):
        half = pl.ds(pl.multiple_of(g * ffh, ffh), ffh)
        part = pl.ds(j * CHUNK, CHUNK)
        return (
            pltpu.make_async_copy(wg_hbm.at[part, half], wg.at[j], wsem.at[0, j]),
            pltpu.make_async_copy(wu_hbm.at[part, half], wu.at[j], wsem.at[1, j]),
            pltpu.make_async_copy(wd_hbm.at[half, part], wd.at[j], wsem.at[2, j]),
        )

    copies = [weight_copies(j) for j in range(nk)]
    for j in range(nk):
        copies[j][0].start()
        copies[j][1].start()
    for j in range(nk):
        copies[j][2].start()

    barrier = pltpu.get_barrier_semaphore()
    for dev in [peer_x, peer_y, peer_c] + [peer_z(p) for p in range(1, outer)]:
        pl.semaphore_signal(barrier, inc=1, device_id=dev, device_id_type=MESH)

    def scale(c0):
        for b in range(c0 // BLOCK, (c0 + CHUNK) // BLOCK):
            cols = slice(b * BLOCK, (b + 1) * BLOCK)
            row = values[:, cols].astype(jnp.float32) * scales[:, b : b + 1]
            zb[zi, :, cols] = row.astype(jnp.bfloat16)

    lane = lax.broadcasted_iota(jnp.int32, (tok, LANES), 1)
    rw = jnp.zeros((tok, LANES), jnp.float32)
    low_lane = jnp.where(lane < 64, lane, lane - 64)
    for k in range(routes.shape[1]):
        rw = rw + jnp.where(low_lane == routes[:, k : k + 1], weights[:, k : k + 1], 0.0)
    high = rw.astype(jnp.bfloat16).astype(jnp.float32)
    zb[zi, :, width:] = jnp.where(lane < 64, high, rw - high).astype(jnp.bfloat16)

    pl.semaphore_wait(barrier, 3 + outer - 1)

    count = [0]
    sent = []

    def move(src, dst, dev):
        n = count[0]
        count[0] += 1
        copy = pltpu.make_async_remote_copy(
            src_ref=src, dst_ref=dst, send_sem=ssem.at[n], recv_sem=rsem.at[n],
            device_id=dev, device_id_type=MESH,
        )
        sent.append(copy)
        return copy

    def landed(view, copy_index):
        pltpu.make_async_remote_copy(
            src_ref=view, dst_ref=view, send_sem=ssem.at[copy_index],
            recv_sem=rsem.at[copy_index], device_id=peer_c, device_id_type=MESH,
        ).wait_recv()

    def block(c, y, xx, c0, c1):
        start = pl.multiple_of((c * 4 + y * 2 + xx) * rows, 16)
        return x.at[pl.ds(start, rows), pl.ds(c0, c1 - c0)]

    def push(view, dev):
        copy = move(view, view, dev)
        copy.start()
        return count[0] - 1

    zid = []
    for c0, c1 in edges:
        ids = []
        scale(c0)
        for p in range(1, outer):
            ids.append(push(zb.at[zi, :, pl.ds(c0, c1 - c0)], peer_z(p)))
        zid.append(ids)
    second, third, fourth = [], [], []

    def gather_line(d):
        c0, c1 = edges[d]
        for p in range(1, outer):
            source = lax.rem(zi - p + outer, outer)
            landed(zb.at[source, :, pl.ds(c0, c1 - c0)], zid[d][p - 1])
        for z in range(outer):
            tmp[z * tok : (z + 1) * tok, : c1 - c0] = zb[z, :, c0:c1].astype(jnp.float32)
        start = pl.multiple_of((ci * 4 + g * 2 + xi) * rows, 16)
        x[pl.ds(start, rows), c0:c1] = tmp[:, : c1 - c0].astype(jnp.bfloat16)
        mine = block(ci, g, xi, c0, c1)
        second.append((push(mine, peer_x), push(mine, peer_y), push(mine, peer_c)))

    def gather_plane(d):
        c0, c1 = edges[d]
        mid = c0 + CHUNK // 2
        landed(block(ci, g, 1 - xi, c0, c1), second[d][0])
        a = push(block(ci, g, 1 - xi, c0, mid), peer_y)
        ca = push(block(ci, g, 1 - xi, c0, c1), peer_c)
        landed(block(ci, 1 - g, xi, c0, c1), second[d][1])
        b = push(block(ci, 1 - g, xi, mid, c1), peer_x)
        cb = push(block(ci, 1 - g, xi, c0, c1), peer_c)
        third.append((a, b, ca, cb))

    def gather_corner(d):
        c0, c1 = edges[d]
        mid = c0 + CHUNK // 2
        landed(block(ci, 1 - g, 1 - xi, c0, mid), third[d][0])
        fa = push(block(ci, 1 - g, 1 - xi, c0, mid), peer_c)
        landed(block(ci, 1 - g, 1 - xi, mid, c1), third[d][1])
        fb = push(block(ci, 1 - g, 1 - xi, mid, c1), peer_c)
        fourth.append((fa, fb))

    def project(d):
        c0, c1 = edges[d]
        mid = c0 + CHUNK // 2
        oc = 1 - ci
        landed(block(oc, g, xi, c0, c1), second[d][2])
        landed(block(oc, g, 1 - xi, c0, c1), third[d][2])
        landed(block(oc, 1 - g, xi, c0, c1), third[d][3])
        landed(block(oc, 1 - g, 1 - xi, c0, mid), fourth[d][0])
        landed(block(oc, 1 - g, 1 - xi, mid, c1), fourth[d][1])
        copies[d][0].wait()
        copies[d][1].wait()

        @pl.loop(0, total // mblk)
        def _(m):
            at = pl.ds(pl.multiple_of(m * mblk, mblk), mblk)
            lhs = x[at, c0 : c0 + CHUNK]

            @pl.loop(0, ffh // ntile)
            def _(n):
                cols = pl.ds(pl.multiple_of(n * ntile, ntile), ntile)
                gate = jnp.dot(lhs, wg[d, :, cols], preferred_element_type=jnp.float32)
                up = jnp.dot(lhs, wu[d, :, cols], preferred_element_type=jnp.float32)
                if d == 0:
                    accg[at, cols] = gate
                    accu[at, cols] = up
                else:
                    accg[at, cols] += gate
                    accu[at, cols] += up

    def run(stages, lag):
        for step in range(nk + (len(stages) - 1) * lag):
            for s, stage in enumerate(stages):
                if 0 <= step - s * lag < nk:
                    stage(step - s * lag)

    run((gather_line, gather_plane, gather_corner, project), GATHER_LAG)

    mine_e = e // group_size

    @pl.loop(0, total // mblk)
    def _(m):
        at = pl.ds(pl.multiple_of(m * mblk, mblk), mblk)
        gate = accg[at, :]
        hid[at, :] = (gate / (1.0 + jnp.exp(-gate)) * accu[at, :]).astype(jnp.bfloat16)
        wide = x[at, width:].astype(jnp.float32)
        lanes = lax.broadcasted_iota(jnp.int32, (mblk, LANES), 1)
        keep = (lanes == mine_e) | (lanes == mine_e + 64)
        column = jnp.sum(jnp.where(keep, wide, 0.0), axis=1, keepdims=True)
        wcol[at, :] = jnp.broadcast_to(column, (mblk, LANES))

    for copy in sent:
        copy.wait_send()
    sent.clear()

    own = pl.ds(pl.multiple_of(ci * 4 * rows, 16), 4 * rows)
    other = pl.ds(pl.multiple_of((1 - ci) * 4 * rows, 16), 4 * rows)
    half = CHUNK // 2
    ids = [dict() for _ in range(nk)]
    dtile = TILE

    def stage_down(j):
        copies[j][2].wait()

        @pl.loop(0, total // mblk)
        def _(m):
            at = pl.ds(pl.multiple_of(m * mblk, mblk), mblk)

            @pl.loop(0, CHUNK // dtile)
            def _(n):
                cols = pl.ds(pl.multiple_of(n * dtile, dtile), dtile)
                to = pl.ds(pl.multiple_of(j * CHUNK + n * dtile, dtile), dtile)
                got = jnp.dot(hid[at, :], wd[j, :, cols], preferred_element_type=jnp.float32)
                x[at, to] = (got * wcol[at, 0:1]).astype(jnp.bfloat16)

        cols = pl.ds(j * CHUNK, CHUNK)
        move(x.at[other, cols], r1.at[:, cols], peer_c).start()
        ids[j]["c"] = count[0] - 1

    def stage_core(j):
        cols = pl.ds(j * CHUNK, CHUNK)
        landed(r1.at[:, cols], ids[j]["c"])
        both = x[own, cols].astype(jnp.float32) + r1[:, cols].astype(jnp.float32)
        r1[:, cols] = both.astype(jnp.bfloat16)
        a, b = pl.ds(j * CHUNK, half), pl.ds(j * CHUNK + half, half)
        h = pl.ds(j * half, half)
        for y in range(2):
            start = pl.multiple_of((y * 2 + 1 - xi) * rows, 16)
            move(r1.at[pl.ds(start, rows), a], r2a.at[y, :, h], peer_x).start()
            ids[j]["x%d" % y] = count[0] - 1
        start = pl.multiple_of((1 - g) * 2 * rows, 16)
        move(r1.at[pl.ds(start, 2 * rows), b], r2b.at[:, h], peer_y).start()
        ids[j]["y"] = count[0] - 1

    def stage_plane(j):
        a, b = pl.ds(j * CHUNK, half), pl.ds(j * CHUNK + half, half)
        h = pl.ds(j * half, half)
        for y in range(2):
            landed(r2a.at[y, :, h], ids[j]["x%d" % y])
            start = pl.multiple_of((y * 2 + xi) * rows, 16)
            both = r1[pl.ds(start, rows), a].astype(jnp.float32) + r2a[y, :, h].astype(jnp.float32)
            r2a[y, :, h] = both.astype(jnp.bfloat16)
        move(r2a.at[1 - g, :, h], r3a.at[:, h], peer_y).start()
        ids[j]["a"] = count[0] - 1
        landed(r2b.at[:, h], ids[j]["y"])
        start = pl.multiple_of(g * 2 * rows, 16)
        both = r1[pl.ds(start, 2 * rows), b].astype(jnp.float32) + r2b[:, h].astype(jnp.float32)
        r2b[:, h] = both.astype(jnp.bfloat16)
        start = pl.multiple_of((1 - xi) * rows, 16)
        move(r2b.at[pl.ds(start, rows), h], r3b.at[:, h], peer_x).start()
        ids[j]["b"] = count[0] - 1

    def stage_line(j):
        h = pl.ds(j * half, half)
        landed(r3a.at[:, h], ids[j]["a"])
        tmp[:, 0:half] = r2a[g, :, h].astype(jnp.float32) + r3a[:, h].astype(jnp.float32)
        landed(r3b.at[:, h], ids[j]["b"])
        start = pl.multiple_of(xi * rows, 16)
        tmp[:, half:CHUNK] = (
            r2b[pl.ds(start, rows), h].astype(jnp.float32) + r3b[:, h].astype(jnp.float32)
        )
        cols = pl.ds(j * CHUNK, CHUNK)
        for z in range(outer):
            zb[z, :, cols] = tmp[z * tok : (z + 1) * tok, 0:CHUNK].astype(jnp.bfloat16)
        ids[j]["z"] = []
        for p in range(1, outer):
            to = lax.rem(zi + p, outer)
            move(zb.at[to, :, cols], zret.at[zi, :, cols], peer_z(p)).start()
            ids[j]["z"].append(count[0] - 1)

    def stage_out(j):
        cols = pl.ds(j * CHUNK, CHUNK)
        sums = zb[zi, :, cols].astype(jnp.float32)
        for p in range(1, outer):
            source = lax.rem(zi - p + outer, outer)
            landed(zret.at[source, :, cols], ids[j]["z"][p - 1])
            sums = sums + zret[source, :, cols].astype(jnp.float32)
        out[:, cols] = sums.astype(jnp.bfloat16)

    run((stage_down, stage_core, stage_plane, stage_line, stage_out), RETURN_LAG)
    for copy in sent:
        copy.wait_send()


def body(values, scales, routes, weights, w_gate, w_up, w_down):
    devices = lax.axis_size("expert")
    outer = devices // 4
    tok, width = values.shape
    ffh = w_gate.shape[1] // 2
    rows = tok * outer
    nk = width // CHUNK
    bf, f32 = jnp.bfloat16, jnp.float32
    n_copies = nk * (outer - 1 + 9) + nk * (6 + outer - 1)
    vmem = pl.BlockSpec(memory_space=pltpu.VMEM)
    hbm = pl.BlockSpec(memory_space=pl.ANY)
    macs = 8 * rows * width * ffh * 3
    return pl.pallas_call(
        functools.partial(kernel, outer, devices // EXPERTS, tok, width, ffh),
        out_shape=jax.ShapeDtypeStruct((tok, width), bf),
        in_specs=[vmem] * 4 + [hbm] * 3,
        out_specs=vmem,
        scratch_shapes=[
            pltpu.VMEM((outer, tok, width + LANES), bf),
            pltpu.VMEM((8 * rows, width + LANES), bf),
            pltpu.VMEM((nk, CHUNK, ffh), bf),
            pltpu.VMEM((nk, CHUNK, ffh), bf),
            pltpu.VMEM((nk, ffh, CHUNK), bf),
            pltpu.VMEM((8 * rows, ffh), f32),
            pltpu.VMEM((8 * rows, ffh), f32),
            pltpu.VMEM((8 * rows, ffh), bf),
            pltpu.VMEM((8 * rows, LANES), f32),
            pltpu.VMEM((rows, CHUNK + LANES), f32),
            pltpu.VMEM((4 * rows, width), bf),
            pltpu.VMEM((2, rows, width // 2), bf),
            pltpu.VMEM((2 * rows, width // 2), bf),
            pltpu.VMEM((rows, width // 2), bf),
            pltpu.VMEM((rows, width // 2), bf),
            pltpu.VMEM((outer, tok, width), bf),
            pltpu.SemaphoreType.DMA((3, nk)),
            pltpu.SemaphoreType.DMA((n_copies,)),
            pltpu.SemaphoreType.DMA((n_copies,)),
        ],
        compiler_params=pltpu.CompilerParams(
            collective_id=0, has_side_effects=True, vmem_limit_bytes=60 * 2**20
        ),
        cost_estimate=pl.CostEstimate(
            flops=2 * macs, bytes_accessed=6 * width * ffh, transcendentals=8 * rows * ffh
        ),
    )(values, scales, routes, weights, w_gate, w_up, w_down)


def solution(mesh):
    return jax.shard_map(
        body,
        mesh=mesh,
        in_specs=(
            P(("group", "expert"), None),
            P(("group", "expert"), None),
            P(("group", "expert"), None),
            P(("group", "expert"), None),
            P(None, "expert"),
            P(None, "expert"),
            P("expert", None),
        ),
        out_specs=P(("group", "expert"), None),
        check_vma=False,
    )
```
